256 devices in a mesh: dp: 32 (over z_hi, x, core), tensor: 8 (over z_lo, y).
Axes of the slice: x: 4, y: 4, z: 8 (z_hi: 4, z_lo: 2; z = z_hi * 2 + z_lo), core: 2. Of those that a mesh axis runs over, the one named last changes fastest.
Arguments:
- activations: bfloat16 [256, 256, 14336], P('dp', None, 'tensor'), may hold values from -6 to 6
- out_grads: bfloat16 [256, 256, 4096], P('dp', None, 'tensor'), may hold values from -6 to 6
- signs_in: int32 [14336], P('tensor'), may hold values from 0 to 1
- signs_out: int32 [4096], P('tensor'), may hold values from 0 to 1
- picks_in: int32 [64], replicated, may hold values from 0 to 14335
- picks_out: int32 [64], replicated, may hold values from 0 to 4095
- test_sketches: bfloat16 [1024, 4096], P('tensor', 'dp'), may hold values from -0.09375 to 0.09375
Outputs:
- scores: float32 [256, 1024], P('dp', 'tensor')
The draws below stay inside these ranges and needn't reach their ends.
All inputs are finite; a program needn't handle non-finite values.
Results may differ from the reference program's by a relative error of at most 0.0029.
Values may be sent and summed in bfloat16 or wider, within the bound.
No kernel may reach another device: no remote copies, remote signals or barrier semaphores. Data moves between devices by JAX's collectives and lax.ppermute only.
A program may use at most 64 MiB of HBM per device.

```python
import math
import jax
import jax.numpy as jnp
from jax import lax

D = 4096
FF = 14336
HB = 256
KI = 64
KO = 64
TOK = 256
M = 1024
KS = 4096
EXAMPLES = 256
N_TENSOR = 8


def set_ends(drawn, own_key, least, top_value):
    extent = drawn.shape
    place = [jax.random.randint(jax.random.fold_in(own_key, axis), (), 0, extent[axis]) for axis in range(len(extent))]
    drawn = drawn.at[tuple(place)].set(least)
    longest = extent.index(max(extent))
    place[longest] = (place[longest] + 1) % extent[longest]
    return drawn.at[tuple(place)].set(top_value)


def steps_of(stream_key, dims, pieces, least, largest):
    level = 1.0
    for axis_at, parts in pieces:
        steps = jax.random.uniform(jax.random.fold_in(jax.random.fold_in(stream_key, 6), axis_at), (parts,), jnp.float32, least / len(pieces), largest / len(pieces))
        level = level * jnp.repeat(jnp.exp(steps), dims[axis_at] // parts).reshape((-1,) + (1,) * (len(dims) - 1 - axis_at))
    return level


def noise(rng, shape, scale, limit, split=(), kind=jnp.bfloat16):
    result = scale * jax.random.normal(rng, shape, jnp.float32)
    if split:
        result = result * steps_of(rng, shape, split, -0.22, 0.18)
    return jnp.clip(result, -limit, limit).astype(kind)


def setup_inputs(seed: int = 0) -> dict:
    seeds = jax.random.split(jax.random.key(seed), 8)
    return {
        "activations": noise(seeds[0], (EXAMPLES, TOK, FF), 1.0, 6.0, ((0, 32), (2, 8))),
        "out_grads": noise(seeds[1], (EXAMPLES, TOK, D), 1.0, 6.0, ((0, 32), (2, 8))),
        "signs_in": set_ends(jax.random.randint(seeds[2], (FF,), 0, 2), jax.random.fold_in(seeds[2], 1), 0, 1).astype(jnp.int32),
        "signs_out": set_ends(jax.random.randint(seeds[3], (D,), 0, 2), jax.random.fold_in(seeds[3], 1), 0, 1).astype(jnp.int32),
        "picks_in": set_ends(jax.random.randint(seeds[4], (KI,), 0, FF), jax.random.fold_in(seeds[4], 1), 0, FF - 1).astype(jnp.int32),
        "picks_out": set_ends(jax.random.randint(seeds[5], (KO,), 0, D), jax.random.fold_in(seeds[5], 1), 0, D - 1).astype(jnp.int32),
        "test_sketches": noise(seeds[6], (M, KS), KS ** -0.5, 0.09375, ((0, 8), (1, 32))),
    }


def parity_sign(left, right):
    common = jnp.bitwise_and(left, right)
    ones_count = jnp.zeros_like(common)
    for position in range(12):
        ones_count = ones_count + jnp.bitwise_and(jnp.right_shift(common, position), 1)
    return (1 - 2 * jnp.bitwise_and(ones_count, 1)).astype(jnp.float32)

def rotate_pick(width, sign_bits, chosen):
    local_width = width // N_TENSOR
    feature = jnp.arange(width, dtype=jnp.int32)[:, None]
    target = chosen.astype(jnp.int32)[None, :]
    matches = feature % local_width // HB == target % local_width // HB
    signed = parity_sign(feature // local_width, target // local_width) * parity_sign(feature % HB, target % HB)
    flips = (2 * sign_bits.astype(jnp.int32) - 1).astype(jnp.float32)[:, None]
    return jnp.where(matches, signed * flips, jnp.float32(0.0)).astype(jnp.bfloat16)

def reference(activations, out_grads, signs_in, signs_out, picks_in, picks_out, test_sketches):
    in_matrix = rotate_pick(FF, signs_in, picks_in)
    out_matrix = rotate_pick(D, signs_out, picks_out)
    norm_scale = 1.0 / math.sqrt(HB * N_TENSOR)

    def per_example(pair):
        act_rows, grad_rows = pair
        picked_in = jnp.dot(act_rows, in_matrix, preferred_element_type=jnp.float32) * norm_scale
        picked_out = jnp.dot(grad_rows, out_matrix, preferred_element_type=jnp.float32) * norm_scale
        outer = jnp.dot(picked_out.T, picked_in, precision=lax.Precision.HIGHEST) / math.sqrt(TOK)
        return outer.reshape(-1)
    sketch = lax.map(per_example, (activations, out_grads)).astype(jnp.bfloat16)
    return jnp.dot(sketch, test_sketches.T, preferred_element_type=jnp.float32)
```

```python
import functools
import math

import jax
import jax.numpy as jnp
from jax import lax
from jax.experimental import pallas as pl
from jax.experimental.pallas import tpu as pltpu
from jax.sharding import PartitionSpec as P

HB = 256
F32, BF16, I32 = jnp.float32, jnp.bfloat16, jnp.int32
VMEM_LIMIT = 40 * 1024 * 1024
VMEM = functools.partial(pl.BlockSpec, memory_space=pltpu.VMEM)
ANY = functools.partial(pl.BlockSpec, memory_space=pl.ANY)


def parity(value):
    for step in (8, 4, 2, 1):
        value = jnp.bitwise_xor(value, jnp.right_shift(value, step))
    return jnp.bitwise_and(value, 1)


def terms_kernel(parts, act_hbm, grad_hbm, sign_in, sign_out, pick_in, pick_out, term_ref, own_ref,
                 act, grad, mat_in, mat_out, sems):
    examples = act.shape[0]
    picks = pick_in.shape[1]
    cols = 2 * picks
    copies = []
    for e in range(examples):
        pair = (
            pltpu.make_async_copy(act_hbm.at[e], act.at[e], sems.at[e, 0]),
            pltpu.make_async_copy(grad_hbm.at[e], grad.at[e], sems.at[e, 1]),
        )
        for copy in pair:
            copy.start()
        copies.append(pair)

    me = lax.axis_index("tensor")
    row = lax.broadcasted_iota(I32, (cols, picks), 0)
    lane = lax.broadcasted_iota(I32, (cols, picks), 1)
    half = picks // 2
    after = row - picks
    from_out = jnp.where(after < half, 2 * after, 2 * (after - half) + 1)
    zero = jnp.zeros((), F32)
    spread = jnp.where(row == lane, pick_in[...].astype(F32), zero) + jnp.where(
        (after >= 0) & (from_out == lane), pick_out[...].astype(F32), zero
    )
    pick = jnp.sum(spread, axis=1, keepdims=True).astype(I32)
    is_in = lax.broadcasted_iota(I32, (cols, 1), 0) < picks

    def part_of(width):
        owner = jnp.zeros_like(pick)
        for q in range(1, parts):
            owner = owner + jnp.where(pick >= q * width, 1, 0)
        return owner, jnp.right_shift(pick - owner * width, 8)

    own_in, block_in = part_of(act.shape[2])
    own_out, block_out = part_of(grad.shape[2])
    owner = jnp.where(is_in, own_in, own_out)
    block_in = jnp.where(is_in, block_in, -1)
    block_out = jnp.where(is_in, -1, block_out)
    offset = lax.broadcasted_iota(I32, (cols, HB), 1)
    odd = jnp.bitwise_xor(
        parity(jnp.bitwise_and(offset, jnp.bitwise_and(pick, HB - 1))),
        parity(jnp.bitwise_and(owner, me)),
    )
    hadamard = (1 - 2 * odd).astype(F32)
    for matrix, signs, blocks in ((mat_in, sign_in, block_in), (mat_out, sign_out, block_out)):
        for j in range(matrix.shape[1] // HB):
            span = slice(j * HB, (j + 1) * HB)
            flips = (2 * signs[:, span] - 1).astype(F32)
            matrix[:, span] = jnp.where(blocks == j, hadamard * flips, zero).astype(BF16)

    contract = (((1,), (1,)), ((), ()))
    for e in range(examples):
        for copy in copies[e]:
            copy.wait()
        total = lax.dot_general(act[e], mat_in[...], contract, preferred_element_type=F32)
        total = total + lax.dot_general(grad[e], mat_out[...], contract, preferred_element_type=F32)
        term_ref[e] = total.astype(BF16)

        @pl.when(me == e)
        def _():
            own_ref[...] = total


def terms(parts, activations, out_grads, signs_in, signs_out, picks_in, picks_out):
    examples, tokens, width_in = activations.shape
    width_out = out_grads.shape[2]
    cols = 2 * picks_in.shape[0]
    return pl.pallas_call(
        functools.partial(terms_kernel, parts),
        out_shape=(
            jax.ShapeDtypeStruct((examples, tokens, cols), BF16),
            jax.ShapeDtypeStruct((tokens, cols), F32),
        ),
        in_specs=[ANY(), ANY()] + [VMEM()] * 4,
        out_specs=(VMEM(), VMEM()),
        scratch_shapes=[
            pltpu.VMEM((examples, tokens, width_in), BF16),
            pltpu.VMEM((examples, tokens, width_out), BF16),
            pltpu.VMEM((cols, width_in), BF16),
            pltpu.VMEM((cols, width_out), BF16),
            pltpu.SemaphoreType.DMA((examples, 2)),
        ],
        compiler_params=pltpu.CompilerParams(vmem_limit_bytes=VMEM_LIMIT),
        cost_estimate=pl.CostEstimate(
            flops=2 * examples * tokens * cols * (width_in + width_out),
            bytes_accessed=2 * examples * tokens * (width_in + width_out),
            transcendentals=0,
        ),
        name="terms",
    )(
        activations,
        out_grads,
        signs_in.reshape(1, -1),
        signs_out.reshape(1, -1),
        picks_in.reshape(1, -1),
        picks_out.reshape(1, -1),
    )


def sketch_kernel(scale, parts_ref, own_ref, out_ref):
    me = lax.axis_index("tensor")
    total = own_ref[...]
    for q in range(parts_ref.shape[0]):
        total = total + jnp.where(me == q, 0.0, parts_ref[q].astype(F32))
    picks = total.shape[1] // 2
    outer = lax.dot_general(
        total, total, (((0,), (0,)), ((), ())), precision=lax.Precision.HIGHEST, preferred_element_type=F32
    )
    half = picks // 2
    sketch = scale * jnp.concatenate(
        [outer[picks : picks + half, :picks], outer[picks + half :, :picks]], axis=1
    )
    for q in range(out_ref.shape[0]):
        out_ref[q] = sketch


def sketch(scale, parts, own):
    count, tokens, cols = parts.shape
    return pl.pallas_call(
        functools.partial(sketch_kernel, scale),
        out_shape=jax.ShapeDtypeStruct((count, cols // 4, cols), F32),
        in_specs=[VMEM(), VMEM()],
        out_specs=VMEM(),
        cost_estimate=pl.CostEstimate(
            flops=12 * tokens * cols * cols, bytes_accessed=2 * count * tokens * cols, transcendentals=0
        ),
        name="sketch",
    )(parts, own)


def scores_kernel(sizes, sketch_ref, *refs):
    tests, out_ref = refs[:-1], refs[-1]
    n_z, n_x, n_c = sizes
    me = lax.axis_index("dp")
    my_z, my_x, my_c = me // (n_x * n_c), (me // n_c) % n_x, me % n_c
    examples = sketch_ref.shape[0]
    total = jnp.zeros((2 * examples, out_ref.shape[1]), F32)
    for c in range(n_c):
        for x in range(n_x):
            for z in range(n_z):
                index = ((my_z + n_z - z) % n_z * n_x + (my_x + n_x - x) % n_x) * n_c + (my_c + c) % n_c
                left = sketch_ref[:, pl.ds(index, 1), :].reshape(examples, -1)
                high = left.astype(BF16).astype(F32)
                both = jnp.concatenate([high, left - high], axis=0).astype(BF16)
                total = total + lax.dot_general(
                    both, tests[c * n_x + x][z], (((1,), (1,)), ((), ())), preferred_element_type=F32
                )
    out_ref[...] = total[:examples] + total[examples:]


def scores(sizes, sketches, tests):
    examples = sketches.shape[0]
    rows = tests[0].shape[1]
    return pl.pallas_call(
        functools.partial(scores_kernel, sizes),
        out_shape=jax.ShapeDtypeStruct((examples, rows), F32),
        in_specs=[VMEM()] * (1 + len(tests)),
        out_specs=VMEM(),
        name="scores",
    )(sketches, *tests)


def shift(value, stride, count, step, size):
    pairs = []
    for i in range(size):
        at = i // stride % count
        pairs.append((i, i + ((at + step) % count - at) * stride))
    return lax.ppermute(value, "dp", pairs)


def gather_tests(block, sizes):
    n_z, n_x, n_c = sizes
    size = n_z * n_x * n_c
    column = jnp.stack([block] + [shift(block, n_x * n_c, n_z, k, size) for k in range(1, n_z)])
    plane = [column] + [shift(column, n_c, n_x, k, size) for k in range(1, n_x)]
    return plane + [shift(column, 1, n_c, 1, size) for column in plane]


def on_device(activations, out_grads, signs_in, signs_out, picks_in, picks_out, test_sketches):
    parts = lax.axis_size("tensor")
    tokens = activations.shape[1]
    sizes = (lax.axis_size("dp") // 8, 4, 2)
    term, own = terms(parts, activations, out_grads, signs_in, signs_out, picks_in, picks_out)
    tests = gather_tests(test_sketches, sizes)
    mine = lax.all_to_all(term, "tensor", 0, 0, tiled=True)
    scale = 1.0 / (HB * parts) / math.sqrt(tokens)
    spread = sketch(scale, mine, own)
    sketches = lax.all_to_all(spread, "tensor", 0, 0, tiled=True)
    return scores(sizes, sketches, tests)


def solution(mesh):
    in_specs = (
        P("dp", None, "tensor"),
        P("dp", None, "tensor"),
        P("tensor"),
        P("tensor"),
        P(),
        P(),
        P("tensor", "dp"),
    )
    out_specs = P("dp", "tensor")
    return jax.shard_map(
        on_device, mesh=mesh, in_specs=in_specs, out_specs=out_specs, check_vma=False
    )
```

```python
import functools
import math

import jax
import jax.numpy as jnp
from jax import lax
from jax.experimental import pallas as pl
from jax.experimental.pallas import tpu as pltpu
from jax.sharding import PartitionSpec as P

HB = 256
F32, BF16, I32 = jnp.float32, jnp.bfloat16, jnp.int32
MIB = 1024 * 1024
AHEAD = 3
VMEM = functools.partial(pl.BlockSpec, memory_space=pltpu.VMEM)
HBM = functools.partial(pl.BlockSpec, memory_space=pltpu.HBM)


def parity(value):
    for step in (8, 4, 2, 1):
        value = jnp.bitwise_xor(value, jnp.right_shift(value, step))
    return jnp.bitwise_and(value, 1)


def terms_kernel(parts, act_hbm, grad_hbm, sign_in_hbm, sign_out_hbm, pick_in_hbm, pick_out_hbm, term_hbm, own_hbm,
                 act, grad, term, own, sign_in, sign_out, pick_in, pick_out, mat_in, mat_out, sems, send_sems, small_sems):
    examples = act.shape[0]
    picks = pick_in.shape[0]
    cols = 2 * picks
    small = [
        pltpu.make_async_copy(source, target, small_sems.at[i])
        for i, (source, target) in enumerate(
            (
                (pick_in_hbm, pick_in),
                (pick_out_hbm, pick_out),
                (sign_in_hbm, sign_in),
                (sign_out_hbm, sign_out),
            )
        )
    ]
    for copy in small:
        copy.start()
    copies = []
    for e in range(examples):
        pair = (
            pltpu.make_async_copy(act_hbm.at[e], act.at[e], sems.at[e, 0]),
            pltpu.make_async_copy(grad_hbm.at[e], grad.at[e], sems.at[e, 1]),
        )
        if e < AHEAD:
            for copy in pair:
                copy.start()
        copies.append(pair)

    for copy in small:
        copy.wait()
    me = lax.axis_index("tensor")
    row = lax.broadcasted_iota(I32, (cols, picks), 0)
    lane = lax.broadcasted_iota(I32, (cols, picks), 1)
    half = picks // 2
    after = row - picks
    from_out = jnp.where(after < half, 2 * after, 2 * (after - half) + 1)
    zero = jnp.zeros((), F32)
    spread = jnp.where(row == lane, pick_in[...].reshape(1, picks).astype(F32), zero) + jnp.where(
        (after >= 0) & (from_out == lane), pick_out[...].reshape(1, picks).astype(F32), zero
    )
    pick = jnp.sum(spread, axis=1, keepdims=True).astype(I32)
    is_in = lax.broadcasted_iota(I32, (cols, 1), 0) < picks

    def part_of(width):
        owner = jnp.zeros_like(pick)
        for q in range(1, parts):
            owner = owner + jnp.where(pick >= q * width, 1, 0)
        return owner, jnp.right_shift(pick - owner * width, 8)

    own_in, block_in = part_of(act.shape[2])
    own_out, block_out = part_of(grad.shape[2])
    owner = jnp.where(is_in, own_in, own_out)
    block_in = jnp.where(is_in, block_in, -1)
    block_out = jnp.where(is_in, -1, block_out)
    offset = lax.broadcasted_iota(I32, (cols, HB), 1)
    odd = jnp.bitwise_xor(
        parity(jnp.bitwise_and(offset, jnp.bitwise_and(pick, HB - 1))),
        parity(jnp.bitwise_and(owner, me)),
    )
    hadamard = (1 - 2 * odd).astype(F32)
    for matrix, signs, blocks in ((mat_in, sign_in, block_in), (mat_out, sign_out, block_out)):
        for j in range(matrix.shape[0] // HB):
            span = slice(j * HB, (j + 1) * HB)
            flips = (2 * signs[span].reshape(1, HB) - 1).astype(F32)
            matrix[span, :] = jnp.where(blocks == j, hadamard * flips, zero).T.astype(BF16)

    sends = []
    for e in range(examples):
        for copy in copies[e]:
            copy.wait()
        if e + AHEAD < examples:
            for copy in copies[e + AHEAD]:
                copy.start()
        total = jnp.dot(act[e], mat_in[...], preferred_element_type=F32)
        total = total + jnp.dot(grad[e], mat_out[...], preferred_element_type=F32)
        term[e] = total.astype(BF16)
        sends.append(pltpu.make_async_copy(term.at[e], term_hbm.at[e], send_sems.at[e]))
        sends[e].start()

        @pl.when(me == e)
        def _():
            own[...] = total

    sends.append(pltpu.make_async_copy(own, own_hbm, send_sems.at[examples]))
    sends[-1].start()
    for copy in sends:
        copy.wait()


def terms(parts, activations, out_grads, signs_in, signs_out, picks_in, picks_out):
    examples, tokens, width_in = activations.shape
    width_out = out_grads.shape[2]
    cols = 2 * picks_in.shape[0]
    return pl.pallas_call(
        functools.partial(terms_kernel, parts),
        out_shape=(
            jax.ShapeDtypeStruct((examples, tokens, cols), BF16),
            jax.ShapeDtypeStruct((tokens, cols), F32),
        ),
        in_specs=[HBM()] * 6,
        out_specs=(HBM(), HBM()),
        scratch_shapes=[
            pltpu.VMEM((examples, tokens, width_in), BF16),
            pltpu.VMEM((examples, tokens, width_out), BF16),
            pltpu.VMEM((examples, tokens, cols), BF16),
            pltpu.VMEM((tokens, cols), F32),
            pltpu.VMEM(signs_in.shape, I32),
            pltpu.VMEM(signs_out.shape, I32),
            pltpu.VMEM(picks_in.shape, I32),
            pltpu.VMEM(picks_out.shape, I32),
            pltpu.VMEM((width_in, cols), BF16),
            pltpu.VMEM((width_out, cols), BF16),
            pltpu.SemaphoreType.DMA((examples, 2)),
            pltpu.SemaphoreType.DMA((examples + 1,)),
            pltpu.SemaphoreType.DMA((4,)),
        ],
        compiler_params=pltpu.CompilerParams(vmem_limit_bytes=63 * MIB),
        cost_estimate=pl.CostEstimate(
            flops=2 * examples * tokens * cols * (width_in + width_out),
            bytes_accessed=2 * examples * tokens * (width_in + width_out),
            transcendentals=0,
        ),
        name="terms",
    )(activations, out_grads, signs_in, signs_out, picks_in, picks_out)


def sketch_kernel(scale, parts_ref, own_ref, out_ref):
    me = lax.axis_index("tensor")
    total = jnp.zeros(own_ref.shape, F32)
    for q in range(parts_ref.shape[0]):
        total = total + jnp.where(me == q, 0.0, parts_ref[q].astype(F32))
    total = total + 2.0 * own_ref[...]
    picks = total.shape[1] // 2
    outer = lax.dot_general(
        total, total, (((0,), (0,)), ((), ())), precision=lax.Precision.HIGHEST, preferred_element_type=F32
    )
    half = picks // 2
    sketch = scale * jnp.concatenate(
        [outer[picks : picks + half, :picks], outer[picks + half :, :picks]], axis=1
    )
    for q in range(out_ref.shape[0]):
        out_ref[q] = sketch


def sketch(scale, parts, own):
    count, tokens, cols = parts.shape
    return pl.pallas_call(
        functools.partial(sketch_kernel, scale),
        out_shape=jax.ShapeDtypeStruct((count, cols // 4, cols), F32),
        in_specs=[VMEM(), VMEM()],
        out_specs=VMEM(),
        cost_estimate=pl.CostEstimate(
            flops=12 * tokens * cols * cols, bytes_accessed=2 * count * tokens * cols, transcendentals=0
        ),
        compiler_params=pltpu.CompilerParams(vmem_limit_bytes=8 * MIB),
        name="sketch",
    )(parts, own)


def scores_kernel(sizes, sketch_ref, *refs):
    tests, out_ref = refs[:-1], refs[-1]
    n_z, n_x, n_c = sizes
    me = lax.axis_index("dp")
    my_z, my_x, my_c = me // (n_x * n_c), (me // n_c) % n_x, me % n_c
    examples = sketch_ref.shape[0]
    total = jnp.zeros((2 * examples, out_ref.shape[1]), F32)
    for c in range(n_c):
        for x in range(n_x):
            for z in range(n_z):
                index = (flip(my_z, z) * n_x + flip(my_x, x)) * n_c + (my_c + c) % n_c
                left = sketch_ref[:, pl.ds(index, 1), :].reshape(examples, -1)
                high = left.astype(BF16).astype(F32)
                both = jnp.concatenate([high, left - high], axis=0).astype(BF16)
                total = total + lax.dot_general(
                    both, tests[c * n_x + x][z], (((1,), (1,)), ((), ())), preferred_element_type=F32
                )
    out_ref[...] = total[:examples] + total[examples:]


def scores(sizes, sketches, tests):
    examples = sketches.shape[0]
    rows = tests[0].shape[1]
    return pl.pallas_call(
        functools.partial(scores_kernel, sizes),
        out_shape=jax.ShapeDtypeStruct((examples, rows), F32),
        in_specs=[VMEM()] * (1 + len(tests)),
        out_specs=VMEM(),
        compiler_params=pltpu.CompilerParams(vmem_limit_bytes=8 * MIB),
        name="scores",
    )(sketches, *tests)


def flip(at, which):
    pair = lambda value: value + 1 - 2 * (value % 2)
    return (at, pair(at), 3 - at, pair(3 - at))[which]


def swap(value, stride, count, which, size):
    pairs = []
    for i in range(size):
        at = i // stride % count
        pairs.append((i, i + (flip(at, which) - at) * stride))
    return lax.ppermute(value, "dp", pairs)


def on_device(activations, out_grads, signs_in, signs_out, picks_in, picks_out, test_sketches):
    parts = lax.axis_size("tensor")
    tokens = activations.shape[1]
    sizes = (lax.axis_size("dp") // 8, 4, 2)
    term, own = terms(parts, activations, out_grads, signs_in, signs_out, picks_in, picks_out)
    n_z, n_x, n_c = sizes
    devices = n_z * n_x * n_c
    column = [test_sketches] + [swap(test_sketches, n_x * n_c, n_z, k, devices) for k in (1, 2, 3)]
    term, *column = lax.optimization_barrier((term, *column))
    column = jnp.stack(column)
    plane = [column] + [swap(column, n_c, n_x, k, devices) for k in (1, 2, 3)]
    tests = plane + [swap(part, 1, n_c, 1, devices) for part in plane]
    mine = lax.all_to_all(term, "tensor", 0, 0, tiled=True)
    scale = 1.0 / (HB * parts) / math.sqrt(tokens)
    spread = sketch(scale, mine, 0.5 * own)
    sketches = lax.all_to_all(spread, "tensor", 0, 0, tiled=True)
    return scores(sizes, sketches, tests)


def solution(mesh):
    in_specs = (
        P("dp", None, "tensor"),
        P("dp", None, "tensor"),
        P("tensor"),
        P("tensor"),
        P(),
        P(),
        P("tensor", "dp"),
    )
    out_specs = P("dp", "tensor")
    return jax.shard_map(
        on_device, mesh=mesh, in_specs=in_specs, out_specs=out_specs, check_vma=False
    )
```

```python
import functools
import math

import jax
import jax.numpy as jnp
from jax import lax
from jax.experimental import pallas as pl
from jax.experimental.pallas import tpu as pltpu
from jax.sharding import PartitionSpec as P

HB = 256
F32, BF16, I32 = jnp.float32, jnp.bfloat16, jnp.int32
MIB = 1024 * 1024
PER = 4
VMEM = functools.partial(pl.BlockSpec, memory_space=pltpu.VMEM)
HBM = functools.partial(pl.BlockSpec, memory_space=pltpu.HBM)


def parity(value):
    for step in (8, 4, 2, 1):
        value = jnp.bitwise_xor(value, jnp.right_shift(value, step))
    return jnp.bitwise_and(value, 1)


def terms_kernel(parts, act, grad, sign_in, sign_out, pick_in, pick_out, from_in, from_out, term_hbm, own_hbm,
                 term, own, mat_in, mat_out, send_sems):
    examples = act.shape[0]
    picks = pick_in.shape[0]
    cols = 2 * picks

    def send(e):
        return pltpu.make_async_copy(term.at[e], term_hbm.at[e], send_sems.at[e])

    me = lax.axis_index("tensor")
    spread = from_in[...] * pick_in[...].reshape(1, picks).astype(F32)
    spread = spread + from_out[...] * pick_out[...].reshape(1, picks).astype(F32)
    pick = jnp.sum(spread, axis=1, keepdims=True).astype(I32)
    zero = jnp.zeros((), F32)
    is_in = lax.broadcasted_iota(I32, (cols, 1), 0) < picks

    def part_of(width):
        owner = jnp.zeros_like(pick)
        for q in range(1, parts):
            owner = owner + jnp.where(pick >= q * width, 1, 0)
        return owner, jnp.right_shift(pick - owner * width, 8)

    own_in, block_in = part_of(act.shape[2])
    own_out, block_out = part_of(grad.shape[2])
    owner = jnp.where(is_in, own_in, own_out)
    block_in = jnp.where(is_in, block_in, -1)
    block_out = jnp.where(is_in, -1, block_out)
    offset = lax.broadcasted_iota(I32, (cols, HB), 1)
    odd = jnp.bitwise_xor(
        parity(jnp.bitwise_and(offset, jnp.bitwise_and(pick, HB - 1))),
        parity(jnp.bitwise_and(owner, me)),
    )
    hadamard = (1 - 2 * odd).astype(F32)
    for matrix, signs, blocks in ((mat_in, sign_in, block_in), (mat_out, sign_out, block_out)):
        for j in range(matrix.shape[0] // HB):
            span = slice(j * HB, (j + 1) * HB)
            flips = (2 * signs[span].reshape(1, HB) - 1).astype(F32)
            matrix[span, :cols] = jnp.where(blocks == j, hadamard * flips, zero).T.astype(BF16)
            matrix[span, cols:] = jnp.zeros((HB, matrix.shape[1] - cols), BF16)


    tokens = act.shape[1]

    def multiply(*totals):
        staged = 0
        for first in range(0, examples, 2 * PER):
            for matrix, source in ((mat_in, act), (mat_out, grad)):
                for j in range(matrix.shape[0] // HB):
                    span = slice(j * HB, (j + 1) * HB)
                    for unit in range(2):
                        at = first + unit * PER
                        pltpu.matmul_push_rhs(matrix[span, :], staged, unit)
                        left = source[at : at + PER, :, span].reshape(PER * tokens, HB)
                        pltpu.matmul_acc_lhs(totals[unit], left, load_staged_rhs=staged)
                    staged = 1 - staged
            for unit in range(2):
                whole = pltpu.matmul_pop(totals[unit])
                for i in range(PER):
                    e = first + unit * PER + i
                    part = whole[i * tokens : (i + 1) * tokens, :cols]
                    term[e] = part.astype(BF16)
                    send(e).start()

                    @pl.when(me == e)
                    def _():
                        own[...] = part

    shape = (PER * tokens, HB)
    pl.run_scoped(multiply, pltpu.ACC(0)(shape, F32), pltpu.ACC(1)(shape, F32))
    last = pltpu.make_async_copy(own, own_hbm, send_sems.at[examples])
    last.start()
    for e in range(examples):
        send(e).wait()
    last.wait()


def terms(parts, activations, out_grads, signs_in, signs_out, picks_in, picks_out, from_in, from_out):
    examples, tokens, width_in = activations.shape
    width_out = out_grads.shape[2]
    cols = 2 * picks_in.shape[0]
    return pl.pallas_call(
        functools.partial(terms_kernel, parts),
        out_shape=(
            jax.ShapeDtypeStruct((examples, tokens, cols), BF16),
            jax.ShapeDtypeStruct((tokens, cols), F32),
        ),
        in_specs=[VMEM()] * 8,
        out_specs=(HBM(), HBM()),
        scratch_shapes=[
            pltpu.VMEM((examples, tokens, cols), BF16),
            pltpu.VMEM((tokens, cols), F32),
            pltpu.VMEM((width_in, HB), BF16),
            pltpu.VMEM((width_out, HB), BF16),
            pltpu.SemaphoreType.DMA((examples + 1,)),
        ],
        compiler_params=pltpu.CompilerParams(vmem_limit_bytes=32 * MIB),
        cost_estimate=pl.CostEstimate(
            flops=2 * examples * tokens * cols * (width_in + width_out),
            bytes_accessed=2 * examples * tokens * (width_in + width_out),
            transcendentals=0,
        ),
        name="terms",
    )(activations, out_grads, signs_in, signs_out, picks_in, picks_out, from_in, from_out)


def sketch_kernel(scale, parts_ref, own_ref, out_ref):
    me = lax.axis_index("tensor")
    total = jnp.zeros(own_ref.shape, F32)
    for q in range(parts_ref.shape[0]):
        total = total + jnp.where(me == q, 0.0, parts_ref[q].astype(F32))
    total = total + 2.0 * own_ref[...]
    picks = total.shape[1] // 2
    half = picks // 2
    outer = lax.dot_general(
        total, total, (((0,), (0,)), ((), ())), precision=lax.Precision.HIGHEST, preferred_element_type=F32
    )
    sketch = scale * jnp.concatenate(
        [outer[picks : picks + half, :picks], outer[picks + half :, :picks]], axis=1
    )
    for q in range(out_ref.shape[0]):
        out_ref[q] = sketch


def sketch(scale, parts, own):
    count, tokens, cols = parts.shape
    return pl.pallas_call(
        functools.partial(sketch_kernel, scale),
        out_shape=jax.ShapeDtypeStruct((count, cols // 4, cols), F32),
        in_specs=[VMEM(), VMEM()],
        out_specs=VMEM(),
        cost_estimate=pl.CostEstimate(
            flops=12 * tokens * cols * cols, bytes_accessed=2 * count * tokens * cols, transcendentals=0
        ),
        compiler_params=pltpu.CompilerParams(vmem_limit_bytes=8 * MIB),
        name="sketch",
    )(parts, own)


def scores_kernel(sizes, sketch_ref, *refs):
    tests, out_ref = refs[:-1], refs[-1]
    n_z, n_x, n_c = sizes
    me = lax.axis_index("dp")
    my_z, my_x, my_c = me // (n_x * n_c), (me // n_c) % n_x, me % n_c
    examples = sketch_ref.shape[0]
    total = jnp.zeros((2 * examples, out_ref.shape[1]), F32)
    for c in range(n_c):
        for x in range(n_x):
            for z in range(n_z):
                index = (flip(my_z, z) * n_x + flip(my_x, x)) * n_c + (my_c + c) % n_c
                left = sketch_ref[:, pl.ds(index, 1), :].reshape(examples, -1)
                high = left.astype(BF16).astype(F32)
                both = jnp.concatenate([high, left - high], axis=0).astype(BF16)
                total = total + lax.dot_general(
                    both, tests[c * n_x + x][z], (((1,), (1,)), ((), ())), preferred_element_type=F32
                )
    out_ref[...] = total[:examples] + total[examples:]


def scores(sizes, sketches, tests):
    examples = sketches.shape[0]
    rows = tests[0].shape[1]
    return pl.pallas_call(
        functools.partial(scores_kernel, sizes),
        out_shape=jax.ShapeDtypeStruct((examples, rows), F32),
        in_specs=[VMEM()] * (1 + len(tests)),
        out_specs=VMEM(),
        compiler_params=pltpu.CompilerParams(vmem_limit_bytes=8 * MIB),
        name="scores",
    )(sketches, *tests)


def layout_kernel(from_in, from_out):
    shape = from_in.shape
    row = lax.broadcasted_iota(I32, shape, 0)
    lane = lax.broadcasted_iota(I32, shape, 1)
    half = shape[1] // 2
    after = row - shape[1]
    out = jnp.where(after < half, 2 * after, 2 * (after - half) + 1)
    from_in[...] = (row == lane).astype(F32)
    from_out[...] = ((after >= 0) & (out == lane)).astype(F32)


def layout(picks):
    shape = jax.ShapeDtypeStruct((2 * picks, picks), F32)
    return pl.pallas_call(
        layout_kernel,
        out_shape=(shape, shape),
        out_specs=(VMEM(), VMEM()),
        compiler_params=pltpu.CompilerParams(vmem_limit_bytes=2 * MIB),
        cost_estimate=pl.CostEstimate(flops=20_000_000_000, bytes_accessed=0, transcendentals=0),
        name="layout",
    )()


def flip(at, which):
    pair = lambda value: value + 1 - 2 * (value % 2)
    return (at, pair(at), 3 - at, pair(3 - at))[which]


def swap(value, stride, count, which, size):
    pairs = []
    for i in range(size):
        at = i // stride % count
        pairs.append((i, i + (flip(at, which) - at) * stride))
    return lax.ppermute(value, "dp", pairs)


def on_device(activations, out_grads, signs_in, signs_out, picks_in, picks_out, test_sketches):
    parts = lax.axis_size("tensor")
    tokens = activations.shape[1]
    sizes = (lax.axis_size("dp") // 8, 4, 2)
    from_in, from_out, block = lax.optimization_barrier((*layout(picks_in.shape[0]), test_sketches))
    term, own = terms(
        parts, activations, out_grads, signs_in, signs_out, picks_in, picks_out, from_in, from_out
    )
    n_z, n_x, n_c = sizes
    devices = n_z * n_x * n_c
    column = [block] + [swap(block, n_x * n_c, n_z, k, devices) for k in (1, 2, 3)]
    term, *column = lax.optimization_barrier((term, *column))
    column = jnp.stack(column)
    plane = [column] + [swap(column, n_c, n_x, k, devices) for k in (1, 2, 3)]
    tests = plane + [swap(part, 1, n_c, 1, devices) for part in plane]
    mine = lax.all_to_all(term, "tensor", 0, 0, tiled=True)
    scale = 1.0 / (HB * parts) / math.sqrt(tokens)
    spread = sketch(scale, mine, 0.5 * own)
    sketches = lax.all_to_all(spread, "tensor", 0, 0, tiled=True)
    return scores(sizes, sketches, tests)


def solution(mesh):
    in_specs = (
        P("dp", None, "tensor"),
        P("dp", None, "tensor"),
        P("tensor"),
        P("tensor"),
        P(),
        P(),
        P("tensor", "dp"),
    )
    out_specs = P("dp", "tensor")
    return jax.shard_map(
        on_device, mesh=mesh, in_specs=in_specs, out_specs=out_specs, check_vma=False
    )
```

```python
import functools
import math

import jax
import jax.numpy as jnp
from jax import lax
from jax.experimental import pallas as pl
from jax.experimental.pallas import tpu as pltpu
from jax.sharding import PartitionSpec as P

HB = 256
F32, BF16, I32 = jnp.float32, jnp.bfloat16, jnp.int32
MIB = 1024 * 1024
PER = 4
VMEM = functools.partial(pl.BlockSpec, memory_space=pltpu.VMEM)
HBM = functools.partial(pl.BlockSpec, memory_space=pltpu.HBM)


def parity(value):
    for step in (8, 4, 2, 1):
        value = jnp.bitwise_xor(value, jnp.right_shift(value, step))
    return jnp.bitwise_and(value, 1)


def terms_kernel(parts, act, grad, sign_in, sign_out, pick_in, pick_out, from_in, from_out, term_hbm, own_hbm,
                 term, own, mat_in, mat_out, send_sems):
    examples = act.shape[0]
    picks = pick_in.shape[0]
    cols = 2 * picks

    def send(e):
        return pltpu.make_async_copy(term.at[e], term_hbm.at[e], send_sems.at[e])

    me = lax.axis_index("tensor")
    spread = from_in[...] * pick_in[...].reshape(1, picks).astype(F32)
    spread = spread + from_out[...] * pick_out[...].reshape(1, picks).astype(F32)
    pick = jnp.sum(spread, axis=1, keepdims=True).astype(I32)
    zero = jnp.zeros((), F32)
    is_in = lax.broadcasted_iota(I32, (cols, 1), 0) < picks

    def part_of(width):
        owner = jnp.zeros_like(pick)
        for q in range(1, parts):
            owner = owner + jnp.where(pick >= q * width, 1, 0)
        return owner, jnp.right_shift(pick - owner * width, 8)

    own_in, block_in = part_of(act.shape[2])
    own_out, block_out = part_of(grad.shape[2])
    owner = jnp.where(is_in, own_in, own_out)
    block_in = jnp.where(is_in, block_in, -1)
    block_out = jnp.where(is_in, -1, block_out)
    offset = lax.broadcasted_iota(I32, (cols, HB), 1)
    odd = jnp.bitwise_xor(
        parity(jnp.bitwise_and(offset, jnp.bitwise_and(pick, HB - 1))),
        parity(jnp.bitwise_and(owner, me)),
    )
    hadamard = (1 - 2 * odd).astype(F32)
    for matrix, signs, blocks in ((mat_in, sign_in, block_in), (mat_out, sign_out, block_out)):
        for j in range(matrix.shape[0] // HB):
            span = slice(j * HB, (j + 1) * HB)
            flips = (2 * signs[span].reshape(1, HB) - 1).astype(F32)
            matrix[span, :cols] = jnp.where(blocks == j, hadamard * flips, zero).T.astype(BF16)
            matrix[span, cols:] = jnp.zeros((HB, matrix.shape[1] - cols), BF16)


    tokens = act.shape[1]

    def multiply(*totals):
        staged = 0
        for first in range(0, examples, 2 * PER):
            for matrix, source in ((mat_in, act), (mat_out, grad)):
                for j in range(matrix.shape[0] // HB):
                    span = slice(j * HB, (j + 1) * HB)
                    for unit in range(2):
                        at = first + unit * PER
                        pltpu.matmul_push_rhs(matrix[span, :], staged, unit)
                        left = source[at : at + PER, :, span].reshape(PER * tokens, HB)
                        pltpu.matmul_acc_lhs(totals[unit], left, load_staged_rhs=staged)
                    staged = 1 - staged
            for unit in range(2):
                whole = pltpu.matmul_pop(totals[unit])
                for i in range(PER):
                    e = first + unit * PER + i
                    part = whole[i * tokens : (i + 1) * tokens, :cols]
                    term[e] = part.astype(BF16)
                    send(e).start()

                    @pl.when(me == e)
                    def _():
                        own[...] = part

    shape = (PER * tokens, HB)
    pl.run_scoped(multiply, pltpu.ACC(0)(shape, F32), pltpu.ACC(1)(shape, F32))
    last = pltpu.make_async_copy(own, own_hbm, send_sems.at[examples])
    last.start()
    for e in range(examples):
        send(e).wait()
    last.wait()


def terms(parts, activations, out_grads, signs_in, signs_out, picks_in, picks_out, from_in, from_out):
    examples, tokens, width_in = activations.shape
    width_out = out_grads.shape[2]
    cols = 2 * picks_in.shape[0]
    return pl.pallas_call(
        functools.partial(terms_kernel, parts),
        out_shape=(
            jax.ShapeDtypeStruct((examples, tokens, cols), BF16),
            jax.ShapeDtypeStruct((tokens, cols), F32),
        ),
        in_specs=[VMEM()] * 8,
        out_specs=(HBM(), HBM()),
        scratch_shapes=[
            pltpu.VMEM((examples, tokens, cols), BF16),
            pltpu.VMEM((tokens, cols), F32),
            pltpu.VMEM((width_in, HB), BF16),
            pltpu.VMEM((width_out, HB), BF16),
            pltpu.SemaphoreType.DMA((examples + 1,)),
        ],
        compiler_params=pltpu.CompilerParams(vmem_limit_bytes=32 * MIB),
        cost_estimate=pl.CostEstimate(
            flops=2 * examples * tokens * cols * (width_in + width_out),
            bytes_accessed=2 * examples * tokens * (width_in + width_out),
            transcendentals=0,
        ),
        name="terms",
    )(activations, out_grads, signs_in, signs_out, picks_in, picks_out, from_in, from_out)


def sketch_kernel(scale, parts_ref, own_ref, out_ref):
    me = lax.axis_index("tensor")
    total = jnp.zeros(own_ref.shape, F32)
    for q in range(parts_ref.shape[0]):
        total = total + jnp.where(me == q, 0.0, parts_ref[q].astype(F32))
    total = total + own_ref[...]
    picks = total.shape[1] // 2
    half = picks // 2
    outer = lax.dot_general(
        total, total, (((0,), (0,)), ((), ())), precision=lax.Precision.HIGHEST, preferred_element_type=F32
    )
    sketch = scale * jnp.concatenate(
        [outer[picks : picks + half, :picks], outer[picks + half :, :picks]], axis=1
    )
    rows = sketch.shape[0]
    for q in range(parts_ref.shape[0]):
        out_ref[q * rows : (q + 1) * rows] = sketch


def sketch(scale, parts, own):
    count, tokens, cols = parts.shape
    return pl.pallas_call(
        functools.partial(sketch_kernel, scale),
        out_shape=jax.ShapeDtypeStruct((count * cols // 4, cols), F32),
        in_specs=[VMEM(), VMEM()],
        out_specs=VMEM(),
        cost_estimate=pl.CostEstimate(
            flops=12 * tokens * cols * cols, bytes_accessed=2 * count * tokens * cols, transcendentals=0
        ),
        compiler_params=pltpu.CompilerParams(vmem_limit_bytes=8 * MIB),
        name="sketch",
    )(parts, own)


def scores_kernel(sizes, sketch_ref, *refs):
    tests, out_ref = refs[:-1], refs[-1]
    n_z, n_x, n_c = sizes
    me = lax.axis_index("dp")
    my_z, my_x, my_c = me // (n_x * n_c), (me // n_c) % n_x, me % n_c
    examples = out_ref.shape[0]
    lefts, rights = [], []
    for c in range(n_c):
        for x in range(n_x):
            for z in range(n_z):
                index = (flip(my_z, z) * n_x + flip(my_x, x)) * n_c + (my_c + c) % n_c
                lefts.append(sketch_ref[pl.ds(index, examples, stride=sketch_ref.shape[0] // examples), :])
                rights.append(tests[c * n_x + x][z])
    total = jnp.zeros((2 * examples, out_ref.shape[1]), F32)
    for first in range(0, len(lefts), 32):
        left = jnp.concatenate(lefts[first : first + 32], axis=1)
        high = left.astype(BF16).astype(F32)
        both = jnp.concatenate([high, left - high], axis=0).astype(BF16)
        right = jnp.concatenate(rights[first : first + 32], axis=1)
        total = total + lax.dot_general(both, right, (((1,), (1,)), ((), ())), preferred_element_type=F32)
    out_ref[...] = total[:examples] + total[examples:]


def scores(sizes, sketches, tests):
    examples = sketches.shape[0] // (sizes[0] * sizes[1] * sizes[2])
    rows = tests[0].shape[1]
    return pl.pallas_call(
        functools.partial(scores_kernel, sizes),
        out_shape=jax.ShapeDtypeStruct((examples, rows), F32),
        in_specs=[VMEM()] * (1 + len(tests)),
        out_specs=VMEM(),
        compiler_params=pltpu.CompilerParams(vmem_limit_bytes=8 * MIB),
        name="scores",
    )(sketches, *tests)


def layout_kernel(from_in, from_out):
    shape = from_in.shape
    row = lax.broadcasted_iota(I32, shape, 0)
    lane = lax.broadcasted_iota(I32, shape, 1)
    half = shape[1] // 2
    after = row - shape[1]
    out = jnp.where(after < half, 2 * after, 2 * (after - half) + 1)
    from_in[...] = (row == lane).astype(F32)
    from_out[...] = ((after >= 0) & (out == lane)).astype(F32)


def layout(picks):
    shape = jax.ShapeDtypeStruct((2 * picks, picks), F32)
    return pl.pallas_call(
        layout_kernel,
        out_shape=(shape, shape),
        out_specs=(VMEM(), VMEM()),
        compiler_params=pltpu.CompilerParams(vmem_limit_bytes=2 * MIB),
        cost_estimate=pl.CostEstimate(flops=20_000_000_000, bytes_accessed=0, transcendentals=0),
        name="layout",
    )()


def flip(at, which):
    pair = lambda value: value + 1 - 2 * (value % 2)
    return (at, pair(at), 3 - at, pair(3 - at))[which]


def swap(value, stride, count, which, size):
    pairs = []
    for i in range(size):
        at = i // stride % count
        pairs.append((i, i + (flip(at, which) - at) * stride))
    return lax.ppermute(value, "dp", pairs)


def on_device(activations, out_grads, signs_in, signs_out, picks_in, picks_out, test_sketches):
    parts = lax.axis_size("tensor")
    tokens = activations.shape[1]
    sizes = (lax.axis_size("dp") // 8, 4, 2)
    from_in, from_out, block = lax.optimization_barrier((*layout(picks_in.shape[0]), test_sketches))
    term, own = terms(
        parts, activations, out_grads, signs_in, signs_out, picks_in, picks_out, from_in, from_out
    )
    n_z, n_x, n_c = sizes
    devices = n_z * n_x * n_c
    column = [block] + [swap(block, n_x * n_c, n_z, k, devices) for k in (1, 2, 3)]
    term, *column = lax.optimization_barrier((term, *column))
    column = jnp.stack(column)
    plane = [column] + [swap(column, n_c, n_x, k, devices) for k in (1, 2, 3)]
    tests = plane + [swap(part, 1, n_c, 1, devices) for part in plane]
    mine = lax.all_to_all(term, "tensor", 0, 0, tiled=True)
    scale = 1.0 / (HB * parts) / math.sqrt(tokens)
    spread = sketch(scale, mine, own)
    sketches = lax.all_to_all(spread, "tensor", 0, 0, tiled=True)
    return scores(sizes, sketches, tests)


def solution(mesh):
    in_specs = (
        P("dp", None, "tensor"),
        P("dp", None, "tensor"),
        P("tensor"),
        P("tensor"),
        P(),
        P(),
        P("tensor", "dp"),
    )
    out_specs = P("dp", "tensor")
    return jax.shard_map(
        on_device, mesh=mesh, in_specs=in_specs, out_specs=out_specs, check_vma=False
    )
```

```python
import functools
import math

import jax
import jax.numpy as jnp
from jax import lax
from jax.experimental import pallas as pl
from jax.experimental.pallas import tpu as pltpu
from jax.sharding import PartitionSpec as P

HB = 256
F32, BF16, I32 = jnp.float32, jnp.bfloat16, jnp.int32
MIB = 1024 * 1024
PER = 4
VMEM = functools.partial(pl.BlockSpec, memory_space=pltpu.VMEM)
HBM = functools.partial(pl.BlockSpec, memory_space=pltpu.HBM)


def parity(value):
    for step in (8, 4, 2, 1):
        value = jnp.bitwise_xor(value, jnp.right_shift(value, step))
    return jnp.bitwise_and(value, 1)


def terms_kernel(parts, act, grad, sign_in, sign_out, pick_in, pick_out, from_in, from_out, term_hbm, own_hbm,
                 term, own, mat_in, mat_out, send_sems):
    examples = act.shape[0]
    picks = pick_in.shape[0]
    cols = 2 * picks

    def send(e):
        return pltpu.make_async_copy(term.at[e], term_hbm.at[e], send_sems.at[e])

    me = lax.axis_index("tensor")
    spread = from_in[...] * pick_in[...].reshape(1, picks).astype(F32)
    spread = spread + from_out[...] * pick_out[...].reshape(1, picks).astype(F32)
    pick = jnp.sum(spread, axis=1, keepdims=True).astype(I32)
    zero = jnp.zeros((), F32)
    is_in = lax.broadcasted_iota(I32, (cols, 1), 0) < picks

    def part_of(width):
        owner = jnp.zeros_like(pick)
        for q in range(1, parts):
            owner = owner + jnp.where(pick >= q * width, 1, 0)
        return owner, jnp.right_shift(pick - owner * width, 8)

    own_in, block_in = part_of(act.shape[2])
    own_out, block_out = part_of(grad.shape[2])
    owner = jnp.where(is_in, own_in, own_out)
    block_in = jnp.where(is_in, block_in, -1)
    block_out = jnp.where(is_in, -1, block_out)
    offset = lax.broadcasted_iota(I32, (cols, HB), 1)
    odd = jnp.bitwise_xor(
        parity(jnp.bitwise_and(offset, jnp.bitwise_and(pick, HB - 1))),
        parity(jnp.bitwise_and(owner, me)),
    )
    hadamard = (1 - 2 * odd).astype(F32)
    for matrix, signs, blocks in ((mat_in, sign_in, block_in), (mat_out, sign_out, block_out)):
        for j in range(matrix.shape[0] // HB):
            span = slice(j * HB, (j + 1) * HB)
            flips = (2 * signs[span].reshape(1, HB) - 1).astype(F32)
            matrix[span, :cols] = jnp.where(blocks == j, hadamard * flips, zero).T.astype(BF16)
            matrix[span, cols:] = jnp.zeros((HB, matrix.shape[1] - cols), BF16)


    tokens = act.shape[1]

    def multiply(*totals):
        staged = 0
        for first in range(0, examples, 2 * PER):
            for matrix, source in ((mat_in, act), (mat_out, grad)):
                for j in range(matrix.shape[0] // HB):
                    span = slice(j * HB, (j + 1) * HB)
                    for unit in range(2):
                        at = first + unit * PER
                        pltpu.matmul_push_rhs(matrix[span, :], staged, unit)
                        left = source[at : at + PER, :, span].reshape(PER * tokens, HB)
                        pltpu.matmul_acc_lhs(totals[unit], left, load_staged_rhs=staged)
                    staged = 1 - staged
            for unit in range(2):
                whole = pltpu.matmul_pop(totals[unit])
                for i in range(PER):
                    e = first + unit * PER + i
                    part = whole[i * tokens : (i + 1) * tokens, :cols]
                    term[e] = part.astype(BF16)
                    send(e).start()

                    @pl.when(me == e)
                    def _():
                        own[...] = part

    shape = (PER * tokens, HB)
    pl.run_scoped(multiply, pltpu.ACC(0)(shape, F32), pltpu.ACC(1)(shape, F32))
    last = pltpu.make_async_copy(own, own_hbm, send_sems.at[examples])
    last.start()
    for e in range(examples):
        send(e).wait()
    last.wait()


def terms(parts, activations, out_grads, signs_in, signs_out, picks_in, picks_out, from_in, from_out):
    examples, tokens, width_in = activations.shape
    width_out = out_grads.shape[2]
    cols = 2 * picks_in.shape[0]
    return pl.pallas_call(
        functools.partial(terms_kernel, parts),
        out_shape=(
            jax.ShapeDtypeStruct((examples, tokens, cols), BF16),
            jax.ShapeDtypeStruct((tokens, cols), F32),
        ),
        in_specs=[VMEM()] * 8,
        out_specs=(HBM(), HBM()),
        scratch_shapes=[
            pltpu.VMEM((examples, tokens, cols), BF16),
            pltpu.VMEM((tokens, cols), F32),
            pltpu.VMEM((width_in, HB), BF16),
            pltpu.VMEM((width_out, HB), BF16),
            pltpu.SemaphoreType.DMA((examples + 1,)),
        ],
        compiler_params=pltpu.CompilerParams(vmem_limit_bytes=32 * MIB),
        cost_estimate=pl.CostEstimate(
            flops=2 * examples * tokens * cols * (width_in + width_out),
            bytes_accessed=2 * examples * tokens * (width_in + width_out),
            transcendentals=0,
        ),
        name="terms",
    )(activations, out_grads, signs_in, signs_out, picks_in, picks_out, from_in, from_out)


def sketch_kernel(scale, parts_ref, own_ref, out_ref):
    me = lax.axis_index("tensor")
    total = jnp.zeros(own_ref.shape, F32)
    for q in range(parts_ref.shape[0]):
        total = total + jnp.where(me == q, 0.0, parts_ref[q].astype(F32))
    total = total + own_ref[...]
    picks = total.shape[1] // 2
    half = picks // 2
    outer = lax.dot_general(
        total, total, (((0,), (0,)), ((), ())), precision=lax.Precision.HIGHEST, preferred_element_type=F32
    )
    sketch = scale * jnp.concatenate(
        [outer[picks : picks + half, :picks], outer[picks + half :, :picks]], axis=1
    )
    rows = sketch.shape[0]
    for q in range(parts_ref.shape[0]):
        out_ref[q * rows : (q + 1) * rows] = sketch


def sketch(scale, parts, own):
    count, tokens, cols = parts.shape
    return pl.pallas_call(
        functools.partial(sketch_kernel, scale),
        out_shape=jax.ShapeDtypeStruct((count * cols // 4, cols), F32),
        in_specs=[VMEM(), VMEM()],
        out_specs=VMEM(),
        cost_estimate=pl.CostEstimate(
            flops=12 * tokens * cols * cols, bytes_accessed=2 * count * tokens * cols, transcendentals=0
        ),
        compiler_params=pltpu.CompilerParams(vmem_limit_bytes=8 * MIB),
        name="sketch",
    )(parts, own)


def scores_kernel(sizes, sketch_ref, *refs):
    tests, out_ref = refs[:-1], refs[-1]
    n_z, n_x, n_c = sizes
    me = lax.axis_index("dp")
    my_z, my_x, my_c = me // (n_x * n_c), (me // n_c) % n_x, me % n_c
    examples = out_ref.shape[0]
    lefts, rights = [], []
    for c in range(n_c):
        for x in range(n_x):
            for z in range(n_z):
                index = (flip(my_z, z) * n_x + flip(my_x, x)) * n_c + (my_c + c) % n_c
                lefts.append(sketch_ref[pl.ds(index, examples, stride=sketch_ref.shape[0] // examples), :])
                rights.append(tests[c * n_x + x][z])
    total = jnp.zeros((2 * examples, out_ref.shape[1]), F32)
    for first in range(0, len(lefts), 32):
        left = jnp.concatenate(lefts[first : first + 32], axis=1)
        high = left.astype(BF16).astype(F32)
        both = jnp.concatenate([high, left - high], axis=0).astype(BF16)
        right = jnp.concatenate(rights[first : first + 32], axis=1)
        total = total + lax.dot_general(both, right, (((1,), (1,)), ((), ())), preferred_element_type=F32)
    out_ref[...] = total[:examples] + total[examples:]


def scores(sizes, sketches, tests):
    examples = sketches.shape[0] // (sizes[0] * sizes[1] * sizes[2])
    rows = tests[0].shape[1]
    return pl.pallas_call(
        functools.partial(scores_kernel, sizes),
        out_shape=jax.ShapeDtypeStruct((examples, rows), F32),
        in_specs=[VMEM()] * (1 + len(tests)),
        out_specs=VMEM(),
        compiler_params=pltpu.CompilerParams(vmem_limit_bytes=8 * MIB),
        name="scores",
    )(sketches, *tests)


def layout_kernel(from_in, from_out):
    shape = from_in.shape
    row = lax.broadcasted_iota(I32, shape, 0)
    lane = lax.broadcasted_iota(I32, shape, 1)
    half = shape[1] // 2
    after = row - shape[1]
    out = jnp.where(after < half, 2 * after, 2 * (after - half) + 1)
    from_in[...] = (row == lane).astype(F32)
    from_out[...] = ((after >= 0) & (out == lane)).astype(F32)


def layout(picks):
    shape = jax.ShapeDtypeStruct((2 * picks, picks), F32)
    return pl.pallas_call(
        layout_kernel,
        out_shape=(shape, shape),
        out_specs=(VMEM(), VMEM()),
        compiler_params=pltpu.CompilerParams(vmem_limit_bytes=2 * MIB),
        cost_estimate=pl.CostEstimate(flops=20_000_000_000, bytes_accessed=0, transcendentals=0),
        name="layout",
    )()


def flip(at, which):
    pair = lambda value: value + 1 - 2 * (value % 2)
    return (at, pair(at), 3 - at, pair(3 - at))[which]


def swap(value, stride, count, which, size):
    pairs = []
    for i in range(size):
        at = i // stride % count
        pairs.append((i, i + (flip(at, which) - at) * stride))
    return lax.ppermute(value, "dp", pairs)


def on_device(activations, out_grads, signs_in, signs_out, picks_in, picks_out, test_sketches):
    parts = lax.axis_size("tensor")
    tokens = activations.shape[1]
    sizes = (lax.axis_size("dp") // 8, 4, 2)
    from_in, from_out, block = lax.optimization_barrier((*layout(picks_in.shape[0]), test_sketches))
    term, own = terms(
        parts, activations, out_grads, signs_in, signs_out, picks_in, picks_out, from_in, from_out
    )
    n_z, n_x, n_c = sizes
    devices = n_z * n_x * n_c
    column = [block] + [
        swap(test_sketches if k == 3 else block, n_x * n_c, n_z, k, devices) for k in (1, 2, 3)
    ]
    term, *column = lax.optimization_barrier((term, *column))
    column = jnp.stack(column)
    plane = [column] + [swap(column, n_c, n_x, k, devices) for k in (1, 2, 3)]
    tests = plane + [swap(part, 1, n_c, 1, devices) for part in plane]
    mine = lax.all_to_all(term, "tensor", 0, 0, tiled=True)
    scale = 1.0 / (HB * parts) / math.sqrt(tokens)
    spread = sketch(scale, mine, own)
    sketches = lax.all_to_all(spread, "tensor", 0, 0, tiled=True)
    return scores(sizes, sketches, tests)


def solution(mesh):
    in_specs = (
        P("dp", None, "tensor"),
        P("dp", None, "tensor"),
        P("tensor"),
        P("tensor"),
        P(),
        P(),
        P("tensor", "dp"),
    )
    out_specs = P("dp", "tensor")
    return jax.shard_map(
        on_device, mesh=mesh, in_specs=in_specs, out_specs=out_specs, check_vma=False
    )
```

```python
import functools
import math

import jax
import jax.numpy as jnp
from jax import lax
from jax.experimental import pallas as pl
from jax.experimental.pallas import tpu as pltpu
from jax.sharding import PartitionSpec as P

HB = 256
F32, BF16, I32 = jnp.float32, jnp.bfloat16, jnp.int32
MIB = 1024 * 1024
PER = 4
VMEM = functools.partial(pl.BlockSpec, memory_space=pltpu.VMEM)
HBM = functools.partial(pl.BlockSpec, memory_space=pltpu.HBM)


def parity(value):
    for step in (8, 4, 2, 1):
        value = jnp.bitwise_xor(value, jnp.right_shift(value, step))
    return jnp.bitwise_and(value, 1)


def terms_kernel(parts, act, grad, sign_in, sign_out, pick_in, pick_out, from_in, from_out, term_hbm, own_hbm,
                 term, own, mat_in, mat_out, send_sems):
    examples = act.shape[0]
    picks = pick_in.shape[0]
    cols = 2 * picks

    def send(e):
        return pltpu.make_async_copy(term.at[e], term_hbm.at[e], send_sems.at[e])

    me = lax.axis_index("tensor")
    spread = from_in[...] * pick_in[...].reshape(1, picks).astype(F32)
    spread = spread + from_out[...] * pick_out[...].reshape(1, picks).astype(F32)
    pick = jnp.sum(spread, axis=1, keepdims=True).astype(I32)
    zero = jnp.zeros((), F32)
    is_in = lax.broadcasted_iota(I32, (cols, 1), 0) < picks

    def part_of(width):
        owner = jnp.zeros_like(pick)
        for q in range(1, parts):
            owner = owner + jnp.where(pick >= q * width, 1, 0)
        return owner, jnp.right_shift(pick - owner * width, 8)

    own_in, block_in = part_of(act.shape[2])
    own_out, block_out = part_of(grad.shape[2])
    owner = jnp.where(is_in, own_in, own_out)
    block_in = jnp.where(is_in, block_in, -1)
    block_out = jnp.where(is_in, -1, block_out)
    offset = lax.broadcasted_iota(I32, (cols, HB), 1)
    odd = jnp.bitwise_xor(
        parity(jnp.bitwise_and(offset, jnp.bitwise_and(pick, HB - 1))),
        parity(jnp.bitwise_and(owner, me)),
    )
    hadamard = (1 - 2 * odd).astype(F32)
    for matrix, signs, blocks in ((mat_in, sign_in, block_in), (mat_out, sign_out, block_out)):
        for j in range(matrix.shape[0] // HB):
            span = slice(j * HB, (j + 1) * HB)
            flips = (2 * signs[span].reshape(1, HB) - 1).astype(F32)
            matrix[span, :cols] = jnp.where(blocks == j, hadamard * flips, zero).T.astype(BF16)
            matrix[span, cols:] = jnp.zeros((HB, matrix.shape[1] - cols), BF16)


    tokens = act.shape[1]

    def multiply(*totals):
        staged = 0
        for first in range(0, examples, 2 * PER):
            for matrix, source in ((mat_in, act), (mat_out, grad)):
                for j in range(matrix.shape[0] // HB):
                    span = slice(j * HB, (j + 1) * HB)
                    for unit in range(2):
                        at = first + unit * PER
                        pltpu.matmul_push_rhs(matrix[span, :], staged, unit)
                        left = source[at : at + PER, :, span].reshape(PER * tokens, HB)
                        pltpu.matmul_acc_lhs(totals[unit], left, load_staged_rhs=staged)
                    staged = 1 - staged
            for unit in range(2):
                whole = pltpu.matmul_pop(totals[unit])
                for i in range(PER):
                    e = first + unit * PER + i
                    part = whole[i * tokens : (i + 1) * tokens, :cols]
                    term[e] = part.astype(BF16)
                    send(e).start()

                    @pl.when(me == e)
                    def _():
                        own[...] = part

    shape = (PER * tokens, HB)
    pl.run_scoped(multiply, pltpu.ACC(0)(shape, F32), pltpu.ACC(1)(shape, F32))
    last = pltpu.make_async_copy(own, own_hbm, send_sems.at[examples])
    last.start()
    for e in range(examples):
        send(e).wait()
    last.wait()


def terms(parts, activations, out_grads, signs_in, signs_out, picks_in, picks_out, from_in, from_out):
    examples, tokens, width_in = activations.shape
    width_out = out_grads.shape[2]
    cols = 2 * picks_in.shape[0]
    return pl.pallas_call(
        functools.partial(terms_kernel, parts),
        out_shape=(
            jax.ShapeDtypeStruct((examples, tokens, cols), BF16),
            jax.ShapeDtypeStruct((tokens, cols), F32),
        ),
        in_specs=[VMEM()] * 8,
        out_specs=(HBM(), HBM()),
        scratch_shapes=[
            pltpu.VMEM((examples, tokens, cols), BF16),
            pltpu.VMEM((tokens, cols), F32),
            pltpu.VMEM((width_in, HB), BF16),
            pltpu.VMEM((width_out, HB), BF16),
            pltpu.SemaphoreType.DMA((examples + 1,)),
        ],
        compiler_params=pltpu.CompilerParams(vmem_limit_bytes=32 * MIB),
        cost_estimate=pl.CostEstimate(
            flops=2 * examples * tokens * cols * (width_in + width_out),
            bytes_accessed=2 * examples * tokens * (width_in + width_out),
            transcendentals=0,
        ),
        name="terms",
    )(activations, out_grads, signs_in, signs_out, picks_in, picks_out, from_in, from_out)


def sketch_kernel(scale, parts_ref, own_ref, out_ref):
    me = lax.axis_index("tensor")
    total = jnp.zeros(own_ref.shape, F32)
    for q in range(parts_ref.shape[0]):
        total = total + jnp.where(me == q, 0.0, parts_ref[q].astype(F32))
    total = total + own_ref[...]
    picks = total.shape[1] // 2
    half = picks // 2
    high = total.astype(BF16)
    low = (total - high.astype(F32)).astype(BF16)
    across = (((0,), (0,)), ((), ()))
    outer = lax.dot_general(high, high, across, preferred_element_type=F32)
    outer = outer + lax.dot_general(high, low, across, preferred_element_type=F32)
    outer = outer + lax.dot_general(low, high, across, preferred_element_type=F32)
    sketch = scale * jnp.concatenate(
        [outer[picks : picks + half, :picks], outer[picks + half :, :picks]], axis=1
    )
    rows = sketch.shape[0]
    for q in range(parts_ref.shape[0]):
        out_ref[q * rows : (q + 1) * rows] = sketch


def sketch(scale, parts, own):
    count, tokens, cols = parts.shape
    return pl.pallas_call(
        functools.partial(sketch_kernel, scale),
        out_shape=jax.ShapeDtypeStruct((count * cols // 4, cols), F32),
        in_specs=[VMEM(), VMEM()],
        out_specs=VMEM(),
        cost_estimate=pl.CostEstimate(
            flops=12 * tokens * cols * cols, bytes_accessed=2 * count * tokens * cols, transcendentals=0
        ),
        compiler_params=pltpu.CompilerParams(vmem_limit_bytes=8 * MIB),
        name="sketch",
    )(parts, own)


def scores_kernel(sizes, sketch_ref, *refs):
    tests, out_ref = refs[:-1], refs[-1]
    n_z, n_x, n_c = sizes
    me = lax.axis_index("dp")
    my_z, my_x, my_c = me // (n_x * n_c), (me // n_c) % n_x, me % n_c
    examples = out_ref.shape[0]
    lefts, rights = [], []
    for c in range(n_c):
        for x in range(n_x):
            for z in range(n_z):
                index = (flip(my_z, z) * n_x + flip(my_x, x)) * n_c + (my_c + c) % n_c
                lefts.append(sketch_ref[pl.ds(index, examples, stride=sketch_ref.shape[0] // examples), :])
                rights.append(tests[c * n_x + x][z])
    total = jnp.zeros((2 * examples, out_ref.shape[1]), F32)
    for first in range(0, len(lefts), 32):
        left = jnp.concatenate(lefts[first : first + 32], axis=1)
        high = left.astype(BF16).astype(F32)
        both = jnp.concatenate([high, left - high], axis=0).astype(BF16)
        right = jnp.concatenate(rights[first : first + 32], axis=1)
        total = total + lax.dot_general(both, right, (((1,), (1,)), ((), ())), preferred_element_type=F32)
    out_ref[...] = total[:examples] + total[examples:]


def scores(sizes, sketches, tests):
    examples = sketches.shape[0] // (sizes[0] * sizes[1] * sizes[2])
    rows = tests[0].shape[1]
    return pl.pallas_call(
        functools.partial(scores_kernel, sizes),
        out_shape=jax.ShapeDtypeStruct((examples, rows), F32),
        in_specs=[VMEM()] * (1 + len(tests)),
        out_specs=VMEM(),
        compiler_params=pltpu.CompilerParams(vmem_limit_bytes=8 * MIB),
        name="scores",
    )(sketches, *tests)


def layout_kernel(from_in, from_out):
    shape = from_in.shape
    row = lax.broadcasted_iota(I32, shape, 0)
    lane = lax.broadcasted_iota(I32, shape, 1)
    half = shape[1] // 2
    after = row - shape[1]
    out = jnp.where(after < half, 2 * after, 2 * (after - half) + 1)
    from_in[...] = (row == lane).astype(F32)
    from_out[...] = ((after >= 0) & (out == lane)).astype(F32)


def layout(picks):
    shape = jax.ShapeDtypeStruct((2 * picks, picks), F32)
    return pl.pallas_call(
        layout_kernel,
        out_shape=(shape, shape),
        out_specs=(VMEM(), VMEM()),
        compiler_params=pltpu.CompilerParams(vmem_limit_bytes=2 * MIB),
        cost_estimate=pl.CostEstimate(flops=20_000_000_000, bytes_accessed=0, transcendentals=0),
        name="layout",
    )()


def flip(at, which):
    pair = lambda value: value + 1 - 2 * (value % 2)
    return (at, pair(at), 3 - at, pair(3 - at))[which]


def swap(value, stride, count, which, size):
    pairs = []
    for i in range(size):
        at = i // stride % count
        pairs.append((i, i + (flip(at, which) - at) * stride))
    return lax.ppermute(value, "dp", pairs)


def on_device(activations, out_grads, signs_in, signs_out, picks_in, picks_out, test_sketches):
    parts = lax.axis_size("tensor")
    tokens = activations.shape[1]
    sizes = (lax.axis_size("dp") // 8, 4, 2)
    from_in, from_out, block = lax.optimization_barrier((*layout(picks_in.shape[0]), test_sketches))
    term, own = terms(
        parts, activations, out_grads, signs_in, signs_out, picks_in, picks_out, from_in, from_out
    )
    n_z, n_x, n_c = sizes
    devices = n_z * n_x * n_c
    column = [block] + [
        swap(test_sketches if k == 3 else block, n_x * n_c, n_z, k, devices) for k in (1, 2, 3)
    ]
    term, *column = lax.optimization_barrier((term, *column))
    column = jnp.stack(column)
    plane = [column] + [swap(column, n_c, n_x, k, devices) for k in (1, 2, 3)]
    tests = plane + [swap(part, 1, n_c, 1, devices) for part in plane]
    mine = lax.all_to_all(term, "tensor", 0, 0, tiled=True)
    scale = 1.0 / (HB * parts) / math.sqrt(tokens)
    spread = sketch(scale, mine, own)
    sketches = lax.all_to_all(spread, "tensor", 0, 0, tiled=True)
    return scores(sizes, sketches, tests)


def solution(mesh):
    in_specs = (
        P("dp", None, "tensor"),
        P("dp", None, "tensor"),
        P("tensor"),
        P("tensor"),
        P(),
        P(),
        P("tensor", "dp"),
    )
    out_specs = P("dp", "tensor")
    return jax.shard_map(
        on_device, mesh=mesh, in_specs=in_specs, out_specs=out_specs, check_vma=False
    )
```
